32 devices in a mesh: dp: 8 (over z, core), cell: 4 (over y, x).
Axes of the slice: x: 2, y: 2, z: 4, core: 2. Of those that a mesh axis runs over, the one named last changes fastest.
Arguments:
- sensitivity: bfloat16 [1536, 8, 4096], P('dp', 'cell'), may hold values from -6 to 6
- kappa: float32 [8, 4096], replicated, may hold values from 0.02 to 0.16
- pick_rows: int32 [8, 16], P('dp'), may hold values from 0 to 191
Outputs:
- data_block: float32 [1536, 128], P('dp', 'cell')
The draws below stay inside these ranges and needn't reach their ends.
Inputs may be any that keep to these rules, and one draw needn't show every extreme that they name: `pick_rows`: row numbers among one index of dp's own data rows; repeats may occur.
All inputs are finite; a program needn't handle non-finite values.
Results may differ from the reference program's by a relative error of at most 0.0023.
Values may be sent and summed in bfloat16 or wider, within the bound.
No kernel may reach another device: no remote copies, remote signals or barrier semaphores. Data moves between devices by JAX's collectives and lax.ppermute only.
A program may use at most 256 MiB of HBM per device.

```python
import math
import jax
import jax.numpy as jnp
from jax import lax

NX = 64
NY = 64
ROWS_DEV = 192
PICK_DEV = 16
PASSES = 2
NZ = 8
NDATA = 1536
PICK = 128
N_DP = 8


def touch_ends(entries, own_key, smallest, largest):
    index_at = [jax.random.randint(jax.random.fold_in(own_key, axis), (), 0, length) for axis, length in enumerate(entries.shape)]
    main_axis = entries.shape.index(max(entries.shape))
    next_to = index_at[:main_axis] + [(index_at[main_axis] + 1) % entries.shape[main_axis]] + index_at[main_axis + 1:]
    return entries.at[tuple(index_at)].set(smallest).at[tuple(next_to)].set(largest)


def block_levels(own_key, extent, cuts, smallest, high):
    gain, own = 1.0, jax.random.fold_in(own_key, 6)
    for dim, blocks in cuts:
        steps = jnp.exp(jax.random.uniform(jax.random.fold_in(own, dim), (blocks,), jnp.float32, smallest / len(cuts), high / len(cuts)))
        gain = gain * jnp.repeat(steps, extent[dim] // blocks).reshape([-1 if axis == dim else 1 for axis in range(len(extent))])
    return gain


def scatter_about(rng, dims, spread, most, split=(), kind=jnp.bfloat16):
    result = jax.random.normal(rng, dims, jnp.float32) * spread
    if len(split) > 0:
        result = block_levels(rng, dims, split, -0.22, 0.18) * result
    return jnp.clip(result, min=-most, max=most).astype(kind)


def setup_inputs(seed: int = 0) -> dict:
    splits = jax.random.split(jax.random.key(seed), 4)
    return {
        "sensitivity": scatter_about(splits[0], (NDATA, NZ, NX * NY), 1.0, 6.0, ((0, 8), (1, 4))),
        "kappa": jnp.clip(jnp.exp(jax.random.uniform(splits[1], (NZ, NX * NY), jnp.float32, math.log(0.02), math.log(0.16))), 0.02, 0.16),
        "pick_rows": touch_ends(jax.random.randint(splits[2], (N_DP, PICK_DEV), 0, ROWS_DEV), jax.random.fold_in(splits[2], 1), 0, ROWS_DEV - 1).astype(jnp.int32),
    }


def plane_neighbours(field):
    plane_size = field.shape[-1]
    shifted_x = jnp.pad(field, ((0, 0), (0, 0), (NY, NY)))
    neighbour_sum = shifted_x[..., 2 * NY:] + shifted_x[..., :-2 * NY]
    shifted_y = jnp.pad(field, ((0, 0), (0, 0), (1, 1)))
    column = jnp.arange(plane_size, dtype=jnp.int32) % NY
    upper = jnp.where(column < NY - 1, shifted_y[..., 2:], 0.0)
    lower = jnp.where(column > 0, shifted_y[..., :-2], 0.0)
    return neighbour_sum + upper + lower

def one_pass(padded, kappa_slab):
    interior = padded[:, 1:-1]
    neighbour_sum = padded[:, 2:] + padded[:, :-2] + plane_neighbours(interior)
    return interior + kappa_slab * (neighbour_sum - 6.0 * interior)

def reference(sensitivity, kappa, pick_rows):
    norm_factor = 1.0 / math.sqrt(NX * NY * NZ)
    chosen_rows = (jnp.arange(N_DP, dtype=jnp.int32)[:, None] * ROWS_DEV + pick_rows).reshape(-1).astype(jnp.int32)
    selected = sensitivity[chosen_rows].reshape(PICK, NZ * NX * NY)
    row_blocks = sensitivity.reshape(N_DP, ROWS_DEV, NZ, NX * NY)

    def smooth_block(block):
        field = block
        for sweep in range(PASSES):
            padded = jnp.pad(field.astype(jnp.float32), ((0, 0), (1, 1), (0, 0)))
            field = one_pass(padded, kappa).astype(jnp.bfloat16)
        rounded = field.reshape(ROWS_DEV, NZ * NX * NY)
        return jnp.dot(rounded, selected.T, preferred_element_type=jnp.float32) * norm_factor
    return lax.map(smooth_block, row_blocks).reshape(NDATA, PICK)
```

```python
import math

import jax
import jax.numpy as jnp
from jax import lax
from jax.sharding import PartitionSpec as P

NY = 64
PASSES = 2


def plane_laplacian(field):
    plane_size = field.shape[-1]
    lanes = [(0, 0)] * (field.ndim - 1)
    shifted_x = jnp.pad(field, lanes + [(NY, NY)])
    shifted_y = jnp.pad(field, lanes + [(1, 1)])
    column = jnp.arange(plane_size, dtype=jnp.int32) % NY
    upper = jnp.where(column < NY - 1, shifted_y[..., 2:], 0.0)
    lower = jnp.where(column > 0, shifted_y[..., :-2], 0.0)
    return shifted_x[..., 2 * NY :] + shifted_x[..., : -2 * NY] + upper + lower - 6.0 * field


def adjoint_pass(field, kappa_planes):
    scaled = field * kappa_planes[:, None]
    return field[1:-1] + plane_laplacian(scaled[1:-1]) + scaled[2:] + scaled[:-2]


def line(pairs):
    return [(2 * a + c, 2 * b + c) for a, b in pairs for c in (0, 1)]


def gather_dp(block):
    count = lax.axis_size("dp")
    chips = count // 2
    chip = lax.axis_index("dp") // 2
    core = lax.axis_index("dp") % 2
    up = down = block
    stack = jnp.zeros((chips,) + block.shape, block.dtype)
    stack = lax.dynamic_update_index_in_dim(stack, block, chip, 0)
    for step in range(1, chips):
        up = lax.ppermute(up, "dp", line([(i, i + 1) for i in range(step - 1, chips - 1)]))
        down = lax.ppermute(down, "dp", line([(i + 1, i) for i in range(0, chips - step)]))
        stack = jnp.where(
            (jnp.arange(chips) == chip - step).reshape((-1,) + (1,) * block.ndim), up[None], stack
        )
        stack = jnp.where(
            (jnp.arange(chips) == chip + step).reshape((-1,) + (1,) * block.ndim), down[None], stack
        )
    other = lax.ppermute(stack, "dp", [(i, i ^ 1) for i in range(count)])
    first = jnp.where(core == 0, stack, other)
    second = jnp.where(core == 0, other, stack)
    return jnp.stack([first, second], axis=1).reshape((count,) + block.shape)


def scatter_sum(parts):
    cells = lax.axis_size("cell")
    cell = lax.axis_index("cell")
    total = lax.dynamic_index_in_dim(parts, cell, 0, False)
    for step in range(1, cells):
        part = lax.dynamic_index_in_dim(parts, lax.rem(cell + step, cells), 0, False)
        total += lax.ppermute(part, "cell", [(i, (i + step) % cells) for i in range(cells)])
    return total


def on_device(sensitivity, kappa, pick_rows):
    row_count, slab_depth, plane_size = sensitivity.shape
    cells = lax.axis_size("cell")
    slab_start = lax.axis_index("cell") * slab_depth
    norm_factor = 1.0 / math.sqrt(plane_size * slab_depth * cells)
    width = PASSES
    picked = jnp.take(sensitivity, pick_rows[0], axis=0, mode="clip").transpose(1, 0, 2)
    before = lax.ppermute(picked[-width:], "cell", [(i, i + 1) for i in range(cells - 1)])
    after = lax.ppermute(picked[:width], "cell", [(i + 1, i) for i in range(cells - 1)])
    field = jnp.concatenate([before, picked, after]).astype(jnp.float32)
    kappa_planes = lax.dynamic_slice_in_dim(
        jnp.pad(kappa, ((width, width), (0, 0))), slab_start, slab_depth + 2 * width, 0
    )
    for sweep in range(PASSES):
        field = adjoint_pass(field, kappa_planes[sweep : kappa_planes.shape[0] - sweep])
    smoothed = field.astype(jnp.bfloat16)
    gathered = gather_dp(smoothed)
    flat = gathered.transpose(0, 2, 1, 3).reshape(-1, slab_depth * plane_size)
    mine = sensitivity.reshape(row_count, slab_depth * plane_size)
    block = jnp.dot(flat, mine.T, preferred_element_type=jnp.float32) * norm_factor
    return scatter_sum(block.reshape(cells, -1, row_count)).T


def solution(mesh):
    placed = (P("dp", "cell", None), P(), P("dp", None))
    return jax.shard_map(
        on_device, mesh=mesh, in_specs=placed, out_specs=P("dp", "cell"), check_vma=False
    )
```

```python
import functools
import math

import jax
import jax.numpy as jnp
from jax import lax
from jax.experimental import pallas as pl
from jax.experimental.pallas import tpu as pltpu
from jax.sharding import PartitionSpec as P

NY = 64
PASSES = 2
VMEM = pl.BlockSpec(memory_space=pltpu.VMEM)
HBM = pl.BlockSpec(memory_space=pltpu.HBM)
SMEM = pl.BlockSpec(memory_space=pltpu.SMEM)


def run_copies(copies):
    for copy in copies:
        copy.start()
    for copy in copies:
        copy.wait()


def pick_kernel(rows_ref, field_ref, out_ref, held, sems):
    rows = held.shape[0]
    run_copies(
        [
            pltpu.make_async_copy(field_ref.at[rows_ref[0, k]], held.at[k], sems.at[k])
            for k in range(rows)
        ]
    )
    run_copies([pltpu.make_async_copy(held, out_ref, sems.at[0])])


def pick(sensitivity, pick_rows):
    rows = pick_rows.shape[-1]
    shape = (rows,) + sensitivity.shape[1:]
    return pl.pallas_call(
        pick_kernel,
        out_shape=jax.ShapeDtypeStruct(shape, sensitivity.dtype),
        in_specs=[SMEM, HBM],
        out_specs=HBM,
        scratch_shapes=[
            pltpu.VMEM(shape, sensitivity.dtype),
            pltpu.SemaphoreType.DMA((rows,)),
        ],
        name="pick",
    )(pick_rows, sensitivity)


def in_plane(field):
    size = field.shape[-1]
    axis = field.ndim - 1
    lane = lax.broadcasted_iota(jnp.int32, field.shape, axis)
    column = lane % NY
    total = jnp.where(lane < size - NY, pltpu.roll(field, size - NY, axis), 0.0)
    total += jnp.where(lane >= NY, pltpu.roll(field, NY, axis), 0.0)
    total += jnp.where(column < NY - 1, pltpu.roll(field, size - 1, axis), 0.0)
    total += jnp.where(column > 0, pltpu.roll(field, 1, axis), 0.0)
    return total


def smooth_kernel(kappa_ref, before_ref, own_ref, after_ref, out_ref, held, ready, sems):
    depth = ready.shape[0]
    run_copies(
        [
            pltpu.make_async_copy(ref, held.at[n], sems.at[n])
            for n, ref in enumerate((before_ref, own_ref, after_ref))
        ]
    )
    planes = []
    for n in range(3):
        block = held[n].astype(jnp.float32)
        planes += [block[:, z] for z in range(block.shape[1])]
    for sweep in range(PASSES):
        scaled = [plane * kappa_ref[sweep + z, :][None] for z, plane in enumerate(planes)]
        planes = [
            planes[z] + (in_plane(scaled[z]) + scaled[z - 1] + scaled[z + 1] - 6.0 * scaled[z])
            for z in range(1, len(planes) - 1)
        ]
    copies = []
    for z in range(depth):
        ready[z] = planes[z].astype(ready.dtype)
        copies.append(pltpu.make_async_copy(ready.at[z], out_ref.at[z], sems.at[z]))
        copies[z].start()
    for copy in copies:
        copy.wait()


def smooth(kappa_planes, before, own, after):
    rows, depth, plane = own.shape
    return pl.pallas_call(
        smooth_kernel,
        out_shape=jax.ShapeDtypeStruct((depth, rows, plane), own.dtype),
        in_specs=[VMEM] + [HBM] * 3,
        out_specs=HBM,
        scratch_shapes=[
            pltpu.VMEM((3,) + own.shape, own.dtype),
            pltpu.VMEM((depth, rows, plane), own.dtype),
            pltpu.SemaphoreType.DMA((max(3, depth),)),
        ],
        compiler_params=pltpu.CompilerParams(vmem_limit_bytes=16 << 20),
        name="smooth",
    )(kappa_planes, before, own, after)


def product_kernel(marks, norm_factor, last, place_ref, mine_ref, *refs):
    chips, chip, core, cell = place_ref[0], place_ref[1], place_ref[2], place_ref[3]
    sums_ref = refs[0] if last else None
    refs = refs[last:]
    sources = sum(len(slot) for slot in marks)
    inputs, outs, stack, sems = refs[:sources], refs[sources:-2 - last], refs[-2 - last], refs[-1 - last]
    total = refs[-1] if last else outs[0]
    slots, depth, rows, plane = stack.shape
    side = 2 * core - 1
    good = jnp.where(core == 0, chip > 0, chip < chips - 1)

    def each(action):
        at = 0
        for n, slot in enumerate(marks):
            for test in slot:
                copy = pltpu.make_async_copy(inputs[at], stack.at[n], sems.at[at])
                at += 1
                if test[3] is None:
                    action(copy)
                else:
                    pl.when(good if test[3] else jnp.logical_not(good))(lambda copy=copy: action(copy))

    each(lambda copy: copy.start())
    if last:
        total[...] = sums_ref[...]
    each(lambda copy: copy.wait())
    value = sum(
        lax.dot_general(
            stack[:, z].reshape(slots * rows, plane), mine_ref[z], (((1,), (1,)), ((), ())),
            preferred_element_type=jnp.float32,
        )
        for z in range(depth)
    )
    for n, slot in enumerate(marks):
        step, turned, other, test = slot[0]
        index = {}
        for name, (turned, other) in {"first": slot[0][1:3], "last": slot[-1][1:3]}.items():
            at = lax.rem(chip + (-side if turned else side) * step + chips, chips)
            index[name] = 2 * at + (1 - core if other else core)
        target = index["first"] if test is None else jnp.where(good, index["first"], index["last"])
        start = pl.multiple_of(target * rows, rows)
        total[pl.ds(start, rows), :] = value[n * rows : (n + 1) * rows] * norm_factor
    if last:
        part = outs[0].shape[0]
        for k, out in enumerate(outs):
            out[...] = total[pl.ds(pl.multiple_of((cell ^ k) * part, part), part), :]


def product(place, mine, sums, slots, outs, norm_factor):
    depth, row_count, plane = mine.shape
    count = lax.axis_size("dp")
    rows = slots[0][0][0].shape[1]
    last = len(sums)
    out = jax.ShapeDtypeStruct((count * rows // outs, row_count), jnp.float32)
    operands = [array for slot in slots for array, _ in slot]
    marks = tuple(tuple(mark for _, mark in slot) for slot in slots)
    need = 2 * (mine.size + len(slots) * depth * rows * plane)
    return pl.pallas_call(
        functools.partial(product_kernel, marks, norm_factor, last),
        out_shape=[out] * outs,
        in_specs=[SMEM] + [VMEM] * (1 + last) + [HBM] * len(operands),
        out_specs=[VMEM] * outs,
        scratch_shapes=[
            pltpu.VMEM((len(slots), depth, rows, plane), mine.dtype),
            pltpu.SemaphoreType.DMA((len(operands),)),
        ]
        + [pltpu.VMEM((count * rows, row_count), jnp.float32)] * last,
        compiler_params=pltpu.CompilerParams(vmem_limit_bytes=need + (8 << 20)),
        name="product",
    )(place, mine, *sums, *operands)


def swap_cores(block):
    return lax.ppermute(block, "dp", [(i, i ^ 1) for i in range(lax.axis_size("dp"))])


def gather_dp(block):
    count = lax.axis_size("dp")
    chips = count // 2
    ring = [(2 * i, 2 * ((i + 1) % chips)) for i in range(chips)]
    ring += [(2 * i + 1, 2 * ((i - 1) % chips) + 1) for i in range(chips)]
    both = [block, swap_cores(block)]
    rounds = [[[(both[0], (0, 0, 0, None))], [(both[1], (0, 0, 1, None))]]]
    for step in range(1, chips // 2 + 1):
        end = 2 * step == chips
        if end and chips == 4:
            pairs = [(2, 4), (4, 6), (5, 3), (3, 1), (0, 2), (1, 0), (6, 7), (7, 5)]
            both = [lax.ppermute(array, "dp", pairs) for array in both]
            turned = [swap_cores(array) for array in both]
            slots = [
                [(both[0], (step, 0, 0, True)), (turned[0], (step, 1, 1, False))],
                [(both[1], (step, 0, 1, True)), (turned[1], (step, 1, 0, False))],
            ]
        else:
            both = [lax.ppermute(array, "dp", ring) for array in both]
            slots = [[(both[0], (step, 0, 0, None))], [(both[1], (step, 0, 1, None))]]
            if not end:
                slots += [
                    [(swap_cores(both[0]), (step, 1, 1, None))],
                    [(swap_cores(both[1]), (step, 1, 0, None))],
                ]
        rounds.append(slots)
    return rounds


def scatter_sum(parts):
    cells = len(parts)
    total = parts[0]
    for step in range(1, cells):
        total += lax.ppermute(parts[step], "cell", [(i, i ^ step) for i in range(cells)])
    return total


def on_device(sensitivity, kappa, pick_rows):
    row_count, slab_depth, plane_size = sensitivity.shape
    cells = lax.axis_size("cell")
    chips = lax.axis_size("dp") // 2
    slab_start = lax.axis_index("cell") * slab_depth
    norm_factor = 1.0 / math.sqrt(plane_size * slab_depth * cells)
    width = PASSES
    place = jnp.stack(
        [chips, lax.axis_index("dp") // 2, lax.axis_index("dp") % 2, lax.axis_index("cell")]
    ).astype(jnp.int32)
    kappa_planes = lax.dynamic_slice_in_dim(
        jnp.pad(kappa, ((width, width), (0, 0))), slab_start, slab_depth + 2 * width, 0
    )
    picked = pick(sensitivity, pick_rows)
    before = lax.ppermute(picked[:, -width:], "cell", [(i, i + 1) for i in range(cells - 1)])
    after = lax.ppermute(picked[:, :width], "cell", [(i + 1, i) for i in range(cells - 1)])
    before, mine = lax.optimization_barrier((before, sensitivity.transpose(1, 0, 2)))
    smoothed = smooth(kappa_planes, before, picked, after)
    rounds = gather_dp(smoothed)
    early = [slot for slots in rounds[:-1] for slot in slots]
    sums = product(place, mine, [], early, 1, norm_factor)
    parts = product(place, mine, sums, rounds[-1], cells, norm_factor)
    return scatter_sum(parts).T


def solution(mesh):
    placed = (P("dp", "cell", None), P(), P("dp", None))
    return jax.shard_map(
        on_device, mesh=mesh, in_specs=placed, out_specs=P("dp", "cell"), check_vma=False
    )
```

```python
import functools
import math

import jax
import jax.numpy as jnp
from jax import lax
from jax.experimental import pallas as pl
from jax.experimental.pallas import tpu as pltpu
from jax.sharding import PartitionSpec as P

NY = 64
PASSES = 2
VMEM = pl.BlockSpec(memory_space=pltpu.VMEM)
HBM = pl.BlockSpec(memory_space=pltpu.HBM)
ANY = pl.BlockSpec(memory_space=pl.ANY)
SMEM = pl.BlockSpec(memory_space=pltpu.SMEM)


def keep(array):
    return pltpu.with_memory_space_constraint(array, pltpu.VMEM)


def spill(array):
    return pltpu.with_memory_space_constraint(array, pltpu.HBM)


def run_copies(copies):
    for copy in copies:
        copy.start()
    for copy in copies:
        copy.wait()


def pick_kernel(rows_ref, field_ref, *refs):
    outs, sems = refs[:-1], refs[-1]
    each = outs[0].shape[0]
    run_copies(
        [
            pltpu.make_async_copy(
                field_ref.at[rows_ref[0, n * each + k]], out.at[k], sems.at[n * each + k]
            )
            for n, out in enumerate(outs)
            for k in range(each)
        ]
    )


def pick(sensitivity, pick_rows):
    rows = pick_rows.shape[-1]
    half = pltpu.VMEM((rows // 2,) + sensitivity.shape[1:], sensitivity.dtype)
    return pl.pallas_call(
        pick_kernel,
        out_shape=[half] * 2,
        in_specs=[SMEM, HBM],
        out_specs=[VMEM] * 2,
        scratch_shapes=[pltpu.SemaphoreType.DMA((rows,))],
        name="pick",
    )(pick_rows, sensitivity)


def halo(halves):
    cells = lax.axis_size("cell")
    first, second = halves
    along = [(i, i ^ 1) for i in range(cells)]
    if cells == 4:
        across = [(i, i ^ 2) for i in range(cells)]
        near_first = lax.ppermute(first, "cell", along)
        via = lax.ppermute(second, "cell", across)
        near_second = lax.ppermute(second, "cell", along)
        far_first = lax.ppermute(near_first, "cell", across)
        far_second = lax.ppermute(via, "cell", along)
    else:
        inner = [(i, i + 1) for i in range(1, cells - 1, 2)]
        inner += [(i + 1, i) for i in range(1, cells - 1, 2)]
        near_first, near_second = [lax.ppermute(half, "cell", along) for half in halves]
        far_first, far_second = [lax.ppermute(half, "cell", inner) for half in halves]
    return (first, near_first, far_first), (second, near_second, far_second)


def in_plane(field):
    size = field.shape[-1]
    axis = field.ndim - 1
    lane = lax.broadcasted_iota(jnp.int32, field.shape, axis)
    column = lane % NY
    total = jnp.where(lane < size - NY, pltpu.roll(field, size - NY, axis), 0.0)
    total += jnp.where(lane >= NY, pltpu.roll(field, NY, axis), 0.0)
    total += jnp.where(column < NY - 1, pltpu.roll(field, size - 1, axis), 0.0)
    total += jnp.where(column > 0, pltpu.roll(field, 1, axis), 0.0)
    return total


def smooth_kernel(place_ref, kappa_ref, *refs):
    out_ref = refs[-1]
    even = lax.rem(place_ref[3], 2) == 0
    results = []
    for n in range(0, len(refs) - 1, 3):
        own, near, far = [ref[...].astype(jnp.float32) for ref in refs[n : n + 3]]
        before, after = jnp.where(even, far, near), jnp.where(even, near, far)
        planes = [block[:, z] for block in (before, own, after) for z in range(own.shape[1])]
        for sweep in range(PASSES):
            scaled = [plane * kappa_ref[sweep + z, :][None] for z, plane in enumerate(planes)]
            planes = [
                planes[z] + (in_plane(scaled[z]) + scaled[z - 1] + scaled[z + 1] - 6.0 * scaled[z])
                for z in range(1, len(planes) - 1)
            ]
        results.append(planes)
    for z in range(out_ref.shape[0]):
        out_ref[z] = jnp.concatenate([planes[z] for planes in results]).astype(out_ref.dtype)


def smooth(place, kappa_planes, groups):
    half, depth, plane = groups[0][0].shape
    operands = [(spill if n == 0 else keep)(array) for group in groups for n, array in enumerate(group)]
    return pl.pallas_call(
        smooth_kernel,
        out_shape=pltpu.VMEM((depth, half * len(groups), plane), groups[0][0].dtype),
        in_specs=[SMEM] + [VMEM] * (1 + len(operands)),
        out_specs=VMEM,
        compiler_params=pltpu.CompilerParams(vmem_limit_bytes=16 << 20),
        name="smooth",
    )(place, kappa_planes, *operands)


def product_kernel(marks, norm_factor, last, place_ref, mine_ref, *refs):
    chips, chip, core, cell = place_ref[0], place_ref[1], place_ref[2], place_ref[3]
    sums_ref = refs[0] if last else None
    refs = refs[last:]
    sources = sum(len(slot) for slot in marks)
    inputs, outs, stack, sems = refs[:sources], refs[sources:-2 - last], refs[-2 - last], refs[-1 - last]
    total = refs[-1] if last else outs[0]
    slots, depth, rows, plane = stack.shape
    side = 2 * core - 1
    good = jnp.where(core == 0, chip > 0, chip < chips - 1)

    def each(action):
        at = 0
        for n, slot in enumerate(marks):
            for test in slot:
                copy = pltpu.make_async_copy(inputs[at], stack.at[n], sems.at[at])
                at += 1
                if test[3] is None:
                    action(copy)
                else:
                    pl.when(good if test[3] else jnp.logical_not(good))(lambda copy=copy: action(copy))

    each(lambda copy: copy.start())
    if last:
        total[...] = sums_ref[...]
    each(lambda copy: copy.wait())
    value = sum(
        lax.dot_general(
            stack[:, z].reshape(slots * rows, plane), mine_ref[z], (((1,), (1,)), ((), ())),
            preferred_element_type=jnp.float32,
        )
        for z in range(depth)
    )
    for n, slot in enumerate(marks):
        step, turned, other, test = slot[0]
        index = {}
        for name, (turned, other) in {"first": slot[0][1:3], "last": slot[-1][1:3]}.items():
            at = lax.rem(chip + (-side if turned else side) * step + chips, chips)
            index[name] = 2 * at + (1 - core if other else core)
        target = index["first"] if test is None else jnp.where(good, index["first"], index["last"])
        start = pl.multiple_of(target * rows, rows)
        total[pl.ds(start, rows), :] = value[n * rows : (n + 1) * rows] * norm_factor
    if last:
        part = outs[0].shape[0]
        for k, out in enumerate(outs):
            start = lax.rem(cell + k, len(outs)) * part
            out[...] = total[pl.ds(pl.multiple_of(start, part), part), :]


def product(place, mine, sums, slots, outs, norm_factor):
    depth, row_count, plane = mine.shape
    count = lax.axis_size("dp")
    rows = slots[0][0][0].shape[1]
    last = len(sums)
    out = pltpu.VMEM((count * rows // outs, row_count), jnp.float32)
    operands = [
        (spill if mark == (0, 0, 1, None) else keep)(array) for slot in slots for array, mark in slot
    ]
    marks = tuple(tuple(mark for _, mark in slot) for slot in slots)
    need = 2 * (mine.size + len(slots) * depth * rows * plane)
    return pl.pallas_call(
        functools.partial(product_kernel, marks, norm_factor, last),
        out_shape=[out] * outs,
        in_specs=[SMEM] + [VMEM] * (1 + last + len(operands)),
        out_specs=[VMEM] * outs,
        scratch_shapes=[
            pltpu.VMEM((len(slots), depth, rows, plane), mine.dtype),
            pltpu.SemaphoreType.DMA((len(operands),)),
        ]
        + [pltpu.VMEM((count * rows, row_count), jnp.float32)] * last,
        compiler_params=pltpu.CompilerParams(vmem_limit_bytes=need + (8 << 20)),
        cost_estimate=pl.CostEstimate(
            flops=2 * len(slots) * rows * row_count * depth * plane,
            bytes_accessed=2 * mine.size,
            transcendentals=0,
        ),
        name="product",
    )(place, mine, *sums, *operands)


def swap_cores(block):
    return lax.ppermute(block, "dp", [(i, i ^ 1) for i in range(lax.axis_size("dp"))])


def first_rounds(block, mine):
    chips = lax.axis_size("dp") // 2
    ring = [(2 * i, 2 * ((i + 1) % chips)) for i in range(chips)]
    ring += [(2 * i + 1, 2 * ((i - 1) % chips) + 1) for i in range(chips)]
    both = [block, swap_cores(block)]
    slots = [[(both[0], (0, 0, 0, None))], [(both[1], (0, 0, 1, None))]]
    for step in range(1, chips // 2):
        both = [lax.ppermute(array, "dp", ring) for array in both]
        if step == 1:
            both[0], mine = lax.optimization_barrier((both[0], mine))
        slots += [[(both[0], (step, 0, 0, None))], [(both[1], (step, 0, 1, None))]]
        slots += [[(swap_cores(both[0]), (step, 1, 1, None))]]
        slots += [[(swap_cores(both[1]), (step, 1, 0, None))]]
    if chips == 4:
        pairs = [(2, 4), (4, 6), (5, 3), (3, 1), (0, 2), (1, 0), (6, 7), (7, 5)]
    else:
        pairs = ring
    return slots, [lax.ppermute(array, "dp", pairs) for array in both], mine


def last_round(both):
    chips = lax.axis_size("dp") // 2
    step = chips // 2
    if chips != 4:
        return [[(both[0], (step, 0, 0, None))], [(both[1], (step, 0, 1, None))]]
    turned = [swap_cores(array) for array in both]
    return [
        [(both[0], (step, 0, 0, True)), (turned[0], (step, 1, 1, False))],
        [(both[1], (step, 0, 1, True)), (turned[1], (step, 1, 0, False))],
    ]


def scatter_sum(parts):
    cells = len(parts)
    total = parts[0]
    for step in range(1, cells):
        total += lax.ppermute(parts[step], "cell", [(i, (i + step) % cells) for i in range(cells)])
    return total


def on_device(sensitivity, kappa, pick_rows):
    row_count, slab_depth, plane_size = sensitivity.shape
    cells = lax.axis_size("cell")
    chips = lax.axis_size("dp") // 2
    slab_start = lax.axis_index("cell") * slab_depth
    norm_factor = 1.0 / math.sqrt(plane_size * slab_depth * cells)
    width = PASSES
    place = jnp.stack(
        [chips, lax.axis_index("dp") // 2, lax.axis_index("dp") % 2, lax.axis_index("cell")]
    ).astype(jnp.int32)
    kappa_planes = lax.dynamic_slice_in_dim(
        jnp.pad(kappa, ((width, width), (0, 0))), slab_start, slab_depth + 2 * width, 0
    )
    smoothed = smooth(place, kappa_planes, halo(pick(sensitivity, pick_rows)))
    smoothed, sensitivity = lax.optimization_barrier((smoothed, sensitivity))
    early, both, mine = first_rounds(smoothed, sensitivity.transpose(1, 0, 2))
    sums = product(place, mine, [], early, 1, norm_factor)
    both[1], sums = lax.optimization_barrier((both[1], sums))
    parts = product(place, mine, sums, last_round(both), cells, norm_factor)
    return scatter_sum(parts).T


def solution(mesh):
    placed = (P("dp", "cell", None), P(), P("dp", None))
    return jax.shard_map(
        on_device, mesh=mesh, in_specs=placed, out_specs=P("dp", "cell"), check_vma=False
    )
```

```python
import functools
import math

import jax
import jax.numpy as jnp
from jax import lax
from jax.experimental import pallas as pl
from jax.experimental.pallas import tpu as pltpu
from jax.sharding import PartitionSpec as P

NY = 64
PASSES = 2
LANES = 128
VMEM = pl.BlockSpec(memory_space=pltpu.VMEM)
HBM = pl.BlockSpec(memory_space=pltpu.HBM)
ANY = pl.BlockSpec(memory_space=pl.ANY)
SMEM = pl.BlockSpec(memory_space=pltpu.SMEM)


def keep(array):
    return pltpu.with_memory_space_constraint(array, pltpu.VMEM)


def spill(array):
    return pltpu.with_memory_space_constraint(array, pltpu.HBM)


def run_copies(copies):
    for copy in copies:
        copy.start()
    for copy in copies:
        copy.wait()


def pick_kernel(rows_ref, field_ref, *refs):
    outs, sems = refs[:-1], refs[-1]
    each = outs[0].shape[0]
    run_copies(
        [
            pltpu.make_async_copy(
                field_ref.at[rows_ref[0, n * each + k]], out.at[k], sems.at[n * each + k]
            )
            for n, out in enumerate(outs)
            for k in range(each)
        ]
    )


def pick(sensitivity, pick_rows):
    rows = pick_rows.shape[-1]
    half = pltpu.VMEM((rows // 2,) + sensitivity.shape[1:], sensitivity.dtype)
    return pl.pallas_call(
        pick_kernel,
        out_shape=[half] * 2,
        in_specs=[SMEM, HBM],
        out_specs=[VMEM] * 2,
        scratch_shapes=[pltpu.SemaphoreType.DMA((rows,))],
        name="pick",
    )(pick_rows, sensitivity)


def halo(halves):
    cells = lax.axis_size("cell")
    first, second = halves
    along = [(i, i ^ 1) for i in range(cells)]
    if cells == 4:
        across = [(i, i ^ 2) for i in range(cells)]
        near_first = lax.ppermute(first, "cell", along)
        via = lax.ppermute(second, "cell", across)
        near_second = lax.ppermute(second, "cell", along)
        far_first = lax.ppermute(near_first, "cell", across)
        far_second = lax.ppermute(via, "cell", along)
    else:
        inner = [(i, i + 1) for i in range(1, cells - 1, 2)]
        inner += [(i + 1, i) for i in range(1, cells - 1, 2)]
        near_first, near_second = [lax.ppermute(half, "cell", along) for half in halves]
        far_first, far_second = [lax.ppermute(half, "cell", inner) for half in halves]
    return (first, near_first, far_first), (second, near_second, far_second)


def in_plane(field):
    rows, size = field.shape
    lane = lax.broadcasted_iota(jnp.int32, (rows, LANES), 1)
    column = lane % NY
    tiles = [field[:, at : at + LANES] for at in range(0, size, LANES)]
    turned = [jnp.zeros((rows, LANES), field.dtype)]
    turned += [pltpu.roll(tile, NY, 1) for tile in tiles]
    turned += turned[:1]
    sums = []
    for n, tile in enumerate(tiles):
        total = turned[n + 1] + jnp.where(lane < NY, turned[n], turned[n + 2])
        total += jnp.where(column < NY - 1, pltpu.roll(tile, LANES - 1, 1), 0.0)
        total += jnp.where(column > 0, pltpu.roll(tile, 1, 1), 0.0)
        sums.append(total)
    return jnp.concatenate(sums, axis=1)


def smooth_kernel(place_ref, kappa_ref, own_ref, near_ref, far_ref, *refs):
    earlier, out_ref = refs[:-1], refs[-1]
    even = lax.rem(place_ref[3], 2) == 0
    own, near, far = [ref[...].astype(jnp.float32) for ref in (own_ref, near_ref, far_ref)]
    before, after = jnp.where(even, far, near), jnp.where(even, near, far)
    planes = [block[:, z] for block in (before, own, after) for z in range(own.shape[1])]
    for sweep in range(PASSES):
        scaled = [plane * kappa_ref[sweep + z, :][None] for z, plane in enumerate(planes)]
        planes = [
            planes[z] + (in_plane(scaled[z]) + scaled[z - 1] + scaled[z + 1] - 6.0 * scaled[z])
            for z in range(1, len(planes) - 1)
        ]
    for z in range(out_ref.shape[0]):
        rows = [planes[z]] + [ref[z] for ref in earlier]
        out_ref[z] = jnp.concatenate(rows).astype(out_ref.dtype)


def smooth(place, kappa_planes, group, earlier, kind):
    half, depth, plane = group[0].shape
    rows = half * (1 + len(earlier))
    operands = [(spill if n == 0 else keep)(array) for n, array in enumerate(group)]
    return pl.pallas_call(
        smooth_kernel,
        out_shape=pltpu.VMEM((depth, rows, plane), kind),
        in_specs=[SMEM] + [VMEM] * (1 + len(operands) + len(earlier)),
        out_specs=VMEM,
        compiler_params=pltpu.CompilerParams(vmem_limit_bytes=16 << 20),
        cost_estimate=pl.CostEstimate(
            flops=100 * half * depth * plane, bytes_accessed=6 * half * depth * plane, transcendentals=0
        ),
        name="smooth",
    )(place, kappa_planes, *operands, *earlier)


def product_kernel(marks, norm_factor, last, depth, place_ref, *refs):
    chips, chip, core, cell = place_ref[0], place_ref[1], place_ref[2], place_ref[3]
    mine, refs = refs[:depth], refs[depth:]
    sums, refs = refs[:last], refs[last:]
    sources = sum(len(slot) for slot in marks)
    inputs, outs = refs[:sources], refs[sources:]
    total = outs[0]
    if last:
        outs, total = outs[:-1], outs[-1]
        total[...] = sums[0][...]
    side = 2 * core - 1
    good = jnp.where(core == 0, chip > 0, chip < chips - 1)
    slots, targets, at = [], [], 0
    for slot in marks:
        refs, at = inputs[at : at + len(slot)], at + len(slot)
        indices = []
        for step, turned, other in slot:
            there = lax.rem(chip + (-side if turned else side) * step + chips, chips)
            indices.append(2 * there + (1 - core if other else core))
        if len(slot) == 1:
            slots.append([refs[0][z] for z in range(depth)])
            targets.append(indices[0])
        else:
            slots.append([jnp.where(good, refs[0][z], refs[1][z]) for z in range(depth)])
            targets.append(jnp.where(good, indices[0], indices[1]))
    value = sum(
        lax.dot_general(
            jnp.concatenate([slot[z] for slot in slots]), mine[z][...], (((1,), (1,)), ((), ())),
            preferred_element_type=jnp.float32,
        )
        for z in range(depth)
    )
    rows = value.shape[0] // len(marks)
    for n, target in enumerate(targets):
        start = pl.multiple_of(target * rows, rows)
        total[pl.ds(start, rows), :] = value[n * rows : (n + 1) * rows] * norm_factor
    if last:
        part = outs[0].shape[0]
        for k, out in enumerate(outs):
            start = lax.rem(cell + k, len(outs)) * part
            out[...] = total[pl.ds(pl.multiple_of(start, part), part), :]


def product(place, mine, sums, slots, outs, norm_factor):
    depth = len(mine)
    row_count, plane = mine[0].shape
    count = lax.axis_size("dp")
    rows = slots[0][0][0].shape[1]
    last = len(sums)
    out = pltpu.VMEM((count * rows // outs, row_count), jnp.float32)
    pairs = [pair for slot in slots for pair in slot]
    operands = [(spill if mark == (0, 0, 1) else keep)(array) for array, mark in pairs]
    marks = tuple(tuple(mark for _, mark in slot) for slot in slots)
    size = depth * plane
    need = 2 * size * (row_count + len(operands) * rows) + 4 * count * rows * row_count
    return pl.pallas_call(
        functools.partial(product_kernel, marks, norm_factor, last, depth),
        out_shape=[out] * outs,
        in_specs=[SMEM] + [VMEM] * (depth + last + len(operands)),
        out_specs=[VMEM] * outs,
        scratch_shapes=[pltpu.VMEM((count * rows, row_count), jnp.float32)] * last,
        compiler_params=pltpu.CompilerParams(vmem_limit_bytes=need + (8 << 20)),
        cost_estimate=pl.CostEstimate(
            flops=2 * len(slots) * rows * row_count * size,
            bytes_accessed=2 * size * row_count,
            transcendentals=0,
        ),
        name="product",
    )(place, *mine, *sums, *operands)


def swap_cores(block):
    return lax.ppermute(block, "dp", [(i, i ^ 1) for i in range(lax.axis_size("dp"))])


def first_rounds(block, mine):
    chips = lax.axis_size("dp") // 2
    ring = [(2 * i, 2 * ((i + 1) % chips)) for i in range(chips)]
    ring += [(2 * i + 1, 2 * ((i - 1) % chips) + 1) for i in range(chips)]
    both = [block, swap_cores(block)]
    slots = [[(both[0], (0, 0, 0))], [(both[1], (0, 0, 1))]]
    turned = []
    for step in range(1, chips // 2):
        both = [lax.ppermute(array, "dp", ring) for array in both]
        if step == 1:
            both[1], mine = lax.optimization_barrier((both[1], mine))
        slots += [[(both[0], (step, 0, 0))], [(both[1], (step, 0, 1))]]
        turned += [[(swap_cores(both[0]), (step, 1, 1))], [(swap_cores(both[1]), (step, 1, 0))]]
    if chips == 4:
        pairs = [(2, 4), (4, 6), (5, 3), (3, 1), (0, 2), (1, 0), (6, 7), (7, 5)]
    else:
        pairs = ring
    return slots, turned, [lax.ppermute(array, "dp", pairs) for array in both], mine


def last_round(both):
    chips = lax.axis_size("dp") // 2
    step = chips // 2
    if chips != 4:
        return [[(both[0], (step, 0, 0))], [(both[1], (step, 0, 1))]]
    turned = [swap_cores(array) for array in both]
    return [
        [(both[0], (step, 0, 0)), (turned[0], (step, 1, 1))],
        [(both[1], (step, 0, 1)), (turned[1], (step, 1, 0))],
    ]


def scatter_sum(parts):
    cells = len(parts)
    total = parts[0]
    for step in range(1, cells):
        total += lax.ppermute(parts[step], "cell", [(i, (i + step) % cells) for i in range(cells)])
    return total


def on_device(sensitivity, kappa, pick_rows):
    row_count, slab_depth, plane_size = sensitivity.shape
    cells = lax.axis_size("cell")
    chips = lax.axis_size("dp") // 2
    slab_start = lax.axis_index("cell") * slab_depth
    norm_factor = 1.0 / math.sqrt(plane_size * slab_depth * cells)
    width = PASSES
    place = jnp.stack(
        [chips, lax.axis_index("dp") // 2, lax.axis_index("dp") % 2, lax.axis_index("cell")]
    ).astype(jnp.int32)
    kappa_planes = lax.dynamic_slice_in_dim(
        jnp.pad(kappa, ((width, width), (0, 0))), slab_start, slab_depth + 2 * width, 0
    )
    first, second = halo(pick(sensitivity, pick_rows))
    half = smooth(place, kappa_planes, second, [], jnp.float32)
    smoothed = smooth(place, kappa_planes, first, [half], sensitivity.dtype)
    smoothed, sensitivity = lax.optimization_barrier((smoothed, sensitivity))
    early, turned, both, mine = first_rounds(smoothed, [sensitivity[:, z] for z in range(slab_depth)])
    sums = product(place, mine, [], early, 1, norm_factor)
    both[1], sums = lax.optimization_barrier((both[1], sums))
    parts = product(place, mine, sums, turned + last_round(both), cells, norm_factor)
    return scatter_sum(parts).T


def solution(mesh):
    placed = (P("dp", "cell"), P(), P("dp"))
    return jax.shard_map(
        on_device, mesh=mesh, in_specs=placed, out_specs=P("dp", "cell"), check_vma=False
    )
```

```python
import functools
import math

import jax
import jax.numpy as jnp
from jax import lax
from jax.experimental import pallas as pl
from jax.experimental.pallas import tpu as pltpu
from jax.sharding import PartitionSpec as P

NY = 64
PASSES = 2
LANES = 128
VMEM = pl.BlockSpec(memory_space=pltpu.VMEM)
HBM = pl.BlockSpec(memory_space=pltpu.HBM)
ANY = pl.BlockSpec(memory_space=pl.ANY)
SMEM = pl.BlockSpec(memory_space=pltpu.SMEM)


def keep(array):
    return pltpu.with_memory_space_constraint(array, pltpu.VMEM)


def spill(array):
    return pltpu.with_memory_space_constraint(array, pltpu.HBM)


def run_copies(copies):
    for copy in copies:
        copy.start()
    for copy in copies:
        copy.wait()


def pick_kernel(rows_ref, field_ref, *refs):
    outs, sems = refs[:-1], refs[-1]
    each = outs[0].shape[0]
    run_copies(
        [
            pltpu.make_async_copy(
                field_ref.at[rows_ref[0, n * each + k]], out.at[k], sems.at[n * each + k]
            )
            for n, out in enumerate(outs)
            for k in range(each)
        ]
    )


def pick(sensitivity, pick_rows):
    rows = pick_rows.shape[-1]
    half = pltpu.VMEM((rows // 2,) + sensitivity.shape[1:], sensitivity.dtype)
    return pl.pallas_call(
        pick_kernel,
        out_shape=[half] * 2,
        in_specs=[SMEM, HBM],
        out_specs=[VMEM] * 2,
        scratch_shapes=[pltpu.SemaphoreType.DMA((rows,))],
        name="pick",
    )(pick_rows, sensitivity)


def halo(halves):
    cells = lax.axis_size("cell")
    first, second = halves
    along = [(i, i ^ 1) for i in range(cells)]
    if cells == 4:
        across = [(i, i ^ 2) for i in range(cells)]
        near_first = lax.ppermute(first, "cell", along)
        via = lax.ppermute(second, "cell", across)
        near_second = lax.ppermute(second, "cell", along)
        far_first = lax.ppermute(near_first, "cell", across)
        far_second = lax.ppermute(via, "cell", along)
    else:
        inner = [(i, i + 1) for i in range(1, cells - 1, 2)]
        inner += [(i + 1, i) for i in range(1, cells - 1, 2)]
        near_first, near_second = [lax.ppermute(half, "cell", along) for half in halves]
        far_first, far_second = [lax.ppermute(half, "cell", inner) for half in halves]
    return (first, near_first, far_first), (second, near_second, far_second)


def in_plane(field):
    rows, size = field.shape
    lane = lax.broadcasted_iota(jnp.int32, (rows, LANES), 1)
    column = lane % NY
    tiles = [field[:, at : at + LANES] for at in range(0, size, LANES)]
    turned = [jnp.zeros((rows, LANES), field.dtype)]
    turned += [pltpu.roll(tile, NY, 1) for tile in tiles]
    turned += turned[:1]
    sums = []
    for n, tile in enumerate(tiles):
        total = turned[n + 1] + jnp.where(lane < NY, turned[n], turned[n + 2])
        total += jnp.where(column < NY - 1, pltpu.roll(tile, LANES - 1, 1), 0.0)
        total += jnp.where(column > 0, pltpu.roll(tile, 1, 1), 0.0)
        sums.append(total)
    return jnp.concatenate(sums, axis=1)


def smooth_kernel(place_ref, kappa_ref, own_ref, near_ref, far_ref, *refs):
    earlier, out_ref = refs[:-1], refs[-1]
    even = lax.rem(place_ref[3], 2) == 0
    own, near, far = [ref[...].astype(jnp.float32) for ref in (own_ref, near_ref, far_ref)]
    before, after = jnp.where(even, far, near), jnp.where(even, near, far)
    planes = [block[:, z] for block in (before, own, after) for z in range(own.shape[1])]
    for sweep in range(PASSES):
        scaled = [plane * kappa_ref[sweep + z, :][None] for z, plane in enumerate(planes)]
        planes = [
            planes[z] + (in_plane(scaled[z]) + scaled[z - 1] + scaled[z + 1] - 6.0 * scaled[z])
            for z in range(1, len(planes) - 1)
        ]
    for z in range(out_ref.shape[0]):
        rows = [planes[z]] + [ref[z] for ref in earlier]
        out_ref[z] = jnp.concatenate(rows).astype(out_ref.dtype)


def smooth(place, kappa_planes, group, earlier, kind):
    half, depth, plane = group[0].shape
    rows = half * (1 + len(earlier))
    operands = [(spill if n == 0 else keep)(array) for n, array in enumerate(group)]
    return pl.pallas_call(
        smooth_kernel,
        out_shape=pltpu.VMEM((depth, rows, plane), kind),
        in_specs=[SMEM] + [VMEM] * (1 + len(operands) + len(earlier)),
        out_specs=VMEM,
        compiler_params=pltpu.CompilerParams(vmem_limit_bytes=16 << 20),
        cost_estimate=pl.CostEstimate(
            flops=100 * half * depth * plane, bytes_accessed=6 * half * depth * plane, transcendentals=0
        ),
        name="smooth",
    )(place, kappa_planes, *operands, *earlier)


def product_kernel(marks, norm_factor, last, place_ref, mine_ref, *refs):
    chips, chip, core, cell = place_ref[0], place_ref[1], place_ref[2], place_ref[3]
    depth = mine_ref.shape[0]
    sums, refs = refs[:last], refs[last:]
    sources = sum(len(slot) for slot in marks)
    inputs, outs = refs[:sources], refs[sources:]
    total = outs[0]
    if last:
        outs, total = outs[:-1], outs[-1]
        total[...] = sums[0][...]
    side = 2 * core - 1
    good = jnp.where(core == 0, chip > 0, chip < chips - 1)
    slots, targets, at = [], [], 0
    for slot in marks:
        refs, at = inputs[at : at + len(slot)], at + len(slot)
        indices = []
        for step, turned, other in slot:
            there = lax.rem(chip + (-side if turned else side) * step + chips, chips)
            indices.append(2 * there + (1 - core if other else core))
        if len(slot) == 1:
            slots.append([refs[0][z] for z in range(depth)])
            targets.append(indices[0])
        else:
            slots.append([jnp.where(good, refs[0][z], refs[1][z]) for z in range(depth)])
            targets.append(jnp.where(good, indices[0], indices[1]))
    value = sum(
        lax.dot_general(
            jnp.concatenate([slot[z] for slot in slots]), mine_ref[z], (((1,), (1,)), ((), ())),
            preferred_element_type=jnp.float32,
        )
        for z in range(depth)
    )
    rows = value.shape[0] // len(marks)
    for n, target in enumerate(targets):
        start = pl.multiple_of(target * rows, rows)
        total[pl.ds(start, rows), :] = value[n * rows : (n + 1) * rows] * norm_factor
    if last:
        part = outs[0].shape[0]
        for k, out in enumerate(outs):
            start = lax.rem(cell + k, len(outs)) * part
            out[...] = total[pl.ds(pl.multiple_of(start, part), part), :]


def product(place, mine, sums, slots, outs, norm_factor):
    depth, row_count, plane = mine.shape
    count = lax.axis_size("dp")
    rows = slots[0][0][0].shape[1]
    last = len(sums)
    out = pltpu.VMEM((count * rows // outs, row_count), jnp.float32)
    pairs = [pair for slot in slots for pair in slot]
    operands = [(spill if mark == (0, 0, 1) else keep)(array) for array, mark in pairs]
    marks = tuple(tuple(mark for _, mark in slot) for slot in slots)
    size = depth * plane
    need = 2 * size * (row_count + len(operands) * rows) + 4 * count * rows * row_count
    return pl.pallas_call(
        functools.partial(product_kernel, marks, norm_factor, last),
        out_shape=[out] * outs,
        in_specs=[SMEM] + [VMEM] * (1 + last + len(operands)),
        out_specs=[VMEM] * outs,
        scratch_shapes=[pltpu.VMEM((count * rows, row_count), jnp.float32)] * last,
        compiler_params=pltpu.CompilerParams(vmem_limit_bytes=need + (8 << 20)),
        cost_estimate=pl.CostEstimate(
            flops=2 * len(slots) * rows * row_count * size,
            bytes_accessed=2 * size * row_count,
            transcendentals=0,
        ),
        name="product",
    )(place, mine, *sums, *operands)


def swap_cores(block):
    return lax.ppermute(block, "dp", [(i, i ^ 1) for i in range(lax.axis_size("dp"))])


def first_rounds(block, mine):
    chips = lax.axis_size("dp") // 2
    ring = [(2 * i, 2 * ((i + 1) % chips)) for i in range(chips)]
    ring += [(2 * i + 1, 2 * ((i - 1) % chips) + 1) for i in range(chips)]
    both = [block, swap_cores(block)]
    slots = [[(both[0], (0, 0, 0))], [(both[1], (0, 0, 1))]]
    turned = []
    for step in range(1, chips // 2):
        both = [lax.ppermute(array, "dp", ring) for array in both]
        if step == 1:
            both[1], mine = lax.optimization_barrier((both[1], mine))
        slots += [[(both[0], (step, 0, 0))], [(both[1], (step, 0, 1))]]
        turned += [[(swap_cores(both[0]), (step, 1, 1))], [(swap_cores(both[1]), (step, 1, 0))]]
    if chips == 4:
        pairs = [(2, 4), (4, 6), (5, 3), (3, 1), (0, 2), (1, 0), (6, 7), (7, 5)]
    else:
        pairs = ring
    return slots, turned, [lax.ppermute(array, "dp", pairs) for array in both], mine


def last_round(both):
    chips = lax.axis_size("dp") // 2
    step = chips // 2
    if chips != 4:
        return [[(both[0], (step, 0, 0))], [(both[1], (step, 0, 1))]]
    turned = [swap_cores(array) for array in both]
    return [
        [(both[0], (step, 0, 0)), (turned[0], (step, 1, 1))],
        [(both[1], (step, 0, 1)), (turned[1], (step, 1, 0))],
    ]


def scatter_sum(parts):
    cells = len(parts)
    total = parts[0]
    for step in range(cells - 1, 0, -1):
        total += lax.ppermute(parts[step], "cell", [(i, (i + step) % cells) for i in range(cells)])
    return total


def on_device(sensitivity, kappa, pick_rows):
    row_count, slab_depth, plane_size = sensitivity.shape
    cells = lax.axis_size("cell")
    chips = lax.axis_size("dp") // 2
    slab_start = lax.axis_index("cell") * slab_depth
    norm_factor = 1.0 / math.sqrt(plane_size * slab_depth * cells)
    width = PASSES
    place = jnp.stack(
        [chips, lax.axis_index("dp") // 2, lax.axis_index("dp") % 2, lax.axis_index("cell")]
    ).astype(jnp.int32)
    kappa_planes = lax.dynamic_slice_in_dim(
        jnp.pad(kappa, ((width, width), (0, 0))), slab_start, slab_depth + 2 * width, 0
    )
    first, second = pick(sensitivity, pick_rows)
    second, kappa_planes = lax.optimization_barrier((second, kappa_planes))
    first, second = halo((first, second))
    half = smooth(place, kappa_planes, second, [], jnp.float32)
    smoothed = smooth(place, kappa_planes, first, [half], sensitivity.dtype)
    smoothed, sensitivity = lax.optimization_barrier((smoothed, sensitivity))
    early, turned, both, mine = first_rounds(smoothed, sensitivity.transpose(1, 0, 2))
    sums = product(place, mine, [], early, 1, norm_factor)
    both[1], sums = lax.optimization_barrier((both[1], sums))
    parts = product(place, mine, sums, turned + last_round(both), cells, norm_factor)
    return scatter_sum(parts).T


def solution(mesh):
    placed = (P("dp", "cell"), P(), P("dp"))
    return jax.shard_map(
        on_device, mesh=mesh, in_specs=placed, out_specs=P("dp", "cell"), check_vma=False
    )
```

```python
import functools
import math

import jax
import jax.numpy as jnp
from jax import lax
from jax.experimental import pallas as pl
from jax.experimental.pallas import tpu as pltpu
from jax.sharding import PartitionSpec as P

NY = 64
PASSES = 2
LANES = 128
VMEM = pl.BlockSpec(memory_space=pltpu.VMEM)
HBM = pl.BlockSpec(memory_space=pltpu.HBM)
ANY = pl.BlockSpec(memory_space=pl.ANY)
SMEM = pl.BlockSpec(memory_space=pltpu.SMEM)


def keep(array):
    return pltpu.with_memory_space_constraint(array, pltpu.VMEM)


def spill(array):
    return pltpu.with_memory_space_constraint(array, pltpu.HBM)


def run_copies(copies):
    for copy in copies:
        copy.start()
    for copy in copies:
        copy.wait()


def pick_kernel(rows_ref, field_ref, *refs):
    outs, sems = refs[:-1], refs[-1]
    each = outs[0].shape[0]
    run_copies(
        [
            pltpu.make_async_copy(
                field_ref.at[rows_ref[0, n * each + k]], out.at[k], sems.at[n * each + k]
            )
            for n, out in enumerate(outs)
            for k in range(each)
        ]
    )


def pick(sensitivity, pick_rows):
    rows = pick_rows.shape[-1]
    half = pltpu.VMEM((rows // 2,) + sensitivity.shape[1:], sensitivity.dtype)
    return pl.pallas_call(
        pick_kernel,
        out_shape=[half] * 2,
        in_specs=[SMEM, HBM],
        out_specs=[VMEM] * 2,
        scratch_shapes=[pltpu.SemaphoreType.DMA((rows,))],
        name="pick",
    )(pick_rows, sensitivity)


def halo(halves):
    cells = lax.axis_size("cell")
    first, second = halves
    along = [(i, i ^ 1) for i in range(cells)]
    if cells == 4:
        across = [(i, i ^ 2) for i in range(cells)]
        near_first = lax.ppermute(first, "cell", along)
        via = lax.ppermute(second, "cell", across)
        near_second = lax.ppermute(second, "cell", along)
        far_first = lax.ppermute(near_first, "cell", across)
        far_second = lax.ppermute(via, "cell", along)
    else:
        inner = [(i, i + 1) for i in range(1, cells - 1, 2)]
        inner += [(i + 1, i) for i in range(1, cells - 1, 2)]
        near_first, near_second = [lax.ppermute(half, "cell", along) for half in halves]
        far_first, far_second = [lax.ppermute(half, "cell", inner) for half in halves]
    return (first, near_first, far_first), (second, near_second, far_second)


def in_plane(field):
    rows, size = field.shape
    lane = lax.broadcasted_iota(jnp.int32, (rows, LANES), 1)
    column = lane % NY
    tiles = [field[:, at : at + LANES] for at in range(0, size, LANES)]
    turned = [jnp.zeros((rows, LANES), field.dtype)]
    turned += [pltpu.roll(tile, NY, 1) for tile in tiles]
    turned += turned[:1]
    sums = []
    for n, tile in enumerate(tiles):
        total = turned[n + 1] + jnp.where(lane < NY, turned[n], turned[n + 2])
        total += jnp.where(column < NY - 1, pltpu.roll(tile, LANES - 1, 1), 0.0)
        total += jnp.where(column > 0, pltpu.roll(tile, 1, 1), 0.0)
        sums.append(total)
    return jnp.concatenate(sums, axis=1)


def smooth_kernel(place_ref, kappa_ref, own_ref, near_ref, far_ref, *refs):
    earlier, out_ref = refs[:-1], refs[-1]
    even = lax.rem(place_ref[3], 2) == 0
    own, near, far = [ref[...].astype(jnp.float32) for ref in (own_ref, near_ref, far_ref)]
    before, after = jnp.where(even, far, near), jnp.where(even, near, far)
    planes = [block[:, z] for block in (before, own, after) for z in range(own.shape[1])]
    for sweep in range(PASSES):
        scaled = [plane * kappa_ref[sweep + z, :][None] for z, plane in enumerate(planes)]
        planes = [
            planes[z] + (in_plane(scaled[z]) + scaled[z - 1] + scaled[z + 1] - 6.0 * scaled[z])
            for z in range(1, len(planes) - 1)
        ]
    for z in range(out_ref.shape[0]):
        rows = [ref[z] for ref in earlier] + [planes[z]]
        out_ref[z] = jnp.concatenate(rows).astype(out_ref.dtype)


def smooth(place, kappa_planes, group, earlier, kind):
    half, depth, plane = group[0].shape
    rows = half * (1 + len(earlier))
    operands = [keep(array) for array in group]
    return pl.pallas_call(
        smooth_kernel,
        out_shape=pltpu.VMEM((depth, rows, plane), kind),
        in_specs=[SMEM] + [VMEM] * (1 + len(operands) + len(earlier)),
        out_specs=VMEM,
        compiler_params=pltpu.CompilerParams(vmem_limit_bytes=16 << 20),
        cost_estimate=pl.CostEstimate(
            flops=100 * half * depth * plane, bytes_accessed=6 * half * depth * plane, transcendentals=0
        ),
        name="smooth",
    )(place, kappa_planes, *operands, *earlier)


def product_kernel(marks, norm_factor, last, place_ref, mine_ref, *refs):
    chips, chip, core, cell = place_ref[0], place_ref[1], place_ref[2], place_ref[3]
    depth = mine_ref.shape[0]
    sums, refs = refs[:last], refs[last:]
    sources = sum(len(slot) for slot in marks)
    inputs, outs = refs[:sources], refs[sources:]
    total = outs[0]
    if last:
        outs, total = outs[:-1], outs[-1]
        total[...] = sums[0][...]
    side = 2 * core - 1
    good = jnp.where(core == 0, chip > 0, chip < chips - 1)
    slots, targets, at = [], [], 0
    for slot in marks:
        refs, at = inputs[at : at + len(slot)], at + len(slot)
        indices = []
        for step, turned, other in slot:
            there = lax.rem(chip + (-side if turned else side) * step + chips, chips)
            indices.append(2 * there + (1 - core if other else core))
        if len(slot) == 1:
            slots.append([refs[0][z] for z in range(depth)])
            targets.append(indices[0])
        else:
            slots.append([jnp.where(good, refs[0][z], refs[1][z]) for z in range(depth)])
            targets.append(jnp.where(good, indices[0], indices[1]))
    value = sum(
        lax.dot_general(
            jnp.concatenate([slot[z] for slot in slots]), mine_ref[z], (((1,), (1,)), ((), ())),
            preferred_element_type=jnp.float32,
        )
        for z in range(depth)
    )
    rows = value.shape[0] // len(marks)
    for n, target in enumerate(targets):
        start = pl.multiple_of(target * rows, rows)
        total[pl.ds(start, rows), :] = value[n * rows : (n + 1) * rows] * norm_factor
    if last:
        part = outs[0].shape[0]
        for k, out in enumerate(outs):
            start = lax.rem(cell + k, len(outs)) * part
            out[...] = total[pl.ds(pl.multiple_of(start, part), part), :]


def product(place, mine, sums, slots, outs, norm_factor):
    depth, row_count, plane = mine.shape
    count = lax.axis_size("dp")
    rows = slots[0][0][0].shape[1]
    last = len(sums)
    out = pltpu.VMEM((count * rows // outs, row_count), jnp.float32)
    pairs = [pair for slot in slots for pair in slot]
    operands = [(spill if mark == (0, 0, 1) else keep)(array) for array, mark in pairs]
    marks = tuple(tuple(mark for _, mark in slot) for slot in slots)
    size = depth * plane
    need = 2 * size * (row_count + len(operands) * rows) + 4 * count * rows * row_count
    return pl.pallas_call(
        functools.partial(product_kernel, marks, norm_factor, last),
        out_shape=[out] * outs,
        in_specs=[SMEM] + [VMEM] * (1 + last + len(operands)),
        out_specs=[VMEM] * outs,
        scratch_shapes=[pltpu.VMEM((count * rows, row_count), jnp.float32)] * last,
        compiler_params=pltpu.CompilerParams(vmem_limit_bytes=need + (8 << 20)),
        cost_estimate=pl.CostEstimate(
            flops=2 * len(slots) * rows * row_count * size,
            bytes_accessed=2 * size * row_count,
            transcendentals=0,
        ),
        name="product",
    )(place, mine, *sums, *operands)


def swap_cores(block):
    return lax.ppermute(block, "dp", [(i, i ^ 1) for i in range(lax.axis_size("dp"))])


def first_rounds(block, mine):
    chips = lax.axis_size("dp") // 2
    ring = [(2 * i, 2 * ((i + 1) % chips)) for i in range(chips)]
    ring += [(2 * i + 1, 2 * ((i - 1) % chips) + 1) for i in range(chips)]
    both = [block, swap_cores(block)]
    slots = [[(both[0], (0, 0, 0))], [(both[1], (0, 0, 1))]]
    turned = []
    for step in range(1, chips // 2):
        both = [lax.ppermute(array, "dp", ring) for array in both]
        if step == 1:
            both[0], mine = lax.optimization_barrier((both[0], mine))
        slots += [[(both[0], (step, 0, 0))], [(both[1], (step, 0, 1))]]
        turned += [[(swap_cores(both[0]), (step, 1, 1))], [(swap_cores(both[1]), (step, 1, 0))]]
    if chips == 4:
        pairs = [(2, 4), (4, 6), (5, 3), (3, 1), (0, 2), (1, 0), (6, 7), (7, 5)]
    else:
        pairs = ring
    return slots, turned, [lax.ppermute(array, "dp", pairs) for array in both], mine


def last_round(both):
    chips = lax.axis_size("dp") // 2
    step = chips // 2
    if chips != 4:
        return [[(both[0], (step, 0, 0))], [(both[1], (step, 0, 1))]]
    turned = [swap_cores(array) for array in both]
    return [
        [(both[0], (step, 0, 0)), (turned[0], (step, 1, 1))],
        [(both[1], (step, 0, 1)), (turned[1], (step, 1, 0))],
    ]


def scatter_sum(parts):
    cells = len(parts)
    total = parts[0]
    for step in range(cells - 1, 0, -1):
        total += lax.ppermute(parts[step], "cell", [(i, (i + step) % cells) for i in range(cells)])
    return total


def on_device(sensitivity, kappa, pick_rows):
    row_count, slab_depth, plane_size = sensitivity.shape
    cells = lax.axis_size("cell")
    chips = lax.axis_size("dp") // 2
    slab_start = lax.axis_index("cell") * slab_depth
    norm_factor = 1.0 / math.sqrt(plane_size * slab_depth * cells)
    width = PASSES
    place = jnp.stack(
        [chips, lax.axis_index("dp") // 2, lax.axis_index("dp") % 2, lax.axis_index("cell")]
    ).astype(jnp.int32)
    kappa_planes = lax.dynamic_slice_in_dim(
        jnp.pad(kappa, ((width, width), (0, 0))), slab_start, slab_depth + 2 * width, 0
    )
    first, second = pick(sensitivity, pick_rows)
    second, kappa_planes = lax.optimization_barrier((second, kappa_planes))
    first, second = halo((first, second))
    half = smooth(place, kappa_planes, first, [], jnp.float32)
    smoothed = smooth(place, kappa_planes, second, [half], sensitivity.dtype)
    smoothed, sensitivity = lax.optimization_barrier((smoothed, sensitivity))
    early, turned, both, mine = first_rounds(smoothed, sensitivity.transpose(1, 0, 2))
    sums = product(place, mine, [], early, 1, norm_factor)
    both[1], sums = lax.optimization_barrier((both[1], sums))
    parts = product(place, mine, sums, turned + last_round(both), cells, norm_factor)
    return scatter_sum(parts).T


def solution(mesh):
    placed = (P("dp", "cell"), P(), P("dp"))
    return jax.shard_map(
        on_device, mesh=mesh, in_specs=placed, out_specs=P("dp", "cell"), check_vma=False
    )
```

```python
import functools
import math

import jax
import jax.numpy as jnp
from jax import lax
from jax.experimental import pallas as pl
from jax.experimental.pallas import tpu as pltpu
from jax.sharding import PartitionSpec as P

NY = 64
PASSES = 2
LANES = 128
VMEM = pl.BlockSpec(memory_space=pltpu.VMEM)
HBM = pl.BlockSpec(memory_space=pltpu.HBM)
ANY = pl.BlockSpec(memory_space=pl.ANY)
SMEM = pl.BlockSpec(memory_space=pltpu.SMEM)


def keep(array):
    return pltpu.with_memory_space_constraint(array, pltpu.VMEM)


def spill(array):
    return pltpu.with_memory_space_constraint(array, pltpu.HBM)


def run_copies(copies):
    for copy in copies:
        copy.start()
    for copy in copies:
        copy.wait()


def pick_kernel(rows_ref, field_ref, *refs):
    outs, sems = refs[:-1], refs[-1]
    each = outs[0].shape[0]
    run_copies(
        [
            pltpu.make_async_copy(
                field_ref.at[rows_ref[0, n * each + k]], out.at[k], sems.at[n * each + k]
            )
            for n, out in enumerate(outs)
            for k in range(each)
        ]
    )


def pick(sensitivity, pick_rows):
    rows = pick_rows.shape[-1]
    half = pltpu.VMEM((rows // 2,) + sensitivity.shape[1:], sensitivity.dtype)
    return pl.pallas_call(
        pick_kernel,
        out_shape=[half] * 2,
        in_specs=[SMEM, HBM],
        out_specs=[VMEM] * 2,
        scratch_shapes=[pltpu.SemaphoreType.DMA((rows,))],
        name="pick",
    )(pick_rows, sensitivity)


def halo(halves):
    cells = lax.axis_size("cell")
    first, second = halves
    along = [(i, i ^ 1) for i in range(cells)]
    if cells == 4:
        across = [(i, i ^ 2) for i in range(cells)]
        near_first = lax.ppermute(first, "cell", along)
        via = lax.ppermute(second, "cell", across)
        near_second = lax.ppermute(second, "cell", along)
        far_first = lax.ppermute(near_first, "cell", across)
        far_second = lax.ppermute(via, "cell", along)
    else:
        inner = [(i, i + 1) for i in range(1, cells - 1, 2)]
        inner += [(i + 1, i) for i in range(1, cells - 1, 2)]
        near_first, near_second = [lax.ppermute(half, "cell", along) for half in halves]
        far_first, far_second = [lax.ppermute(half, "cell", inner) for half in halves]
    return (first, near_first, far_first), (second, near_second, far_second)


def in_plane(field):
    rows, size = field.shape
    lane = lax.broadcasted_iota(jnp.int32, (rows, LANES), 1)
    column = lane % NY
    tiles = [field[:, at : at + LANES] for at in range(0, size, LANES)]
    turned = [jnp.zeros((rows, LANES), field.dtype)]
    turned += [pltpu.roll(tile, NY, 1) for tile in tiles]
    turned += turned[:1]
    sums = []
    for n, tile in enumerate(tiles):
        total = turned[n + 1] + jnp.where(lane < NY, turned[n], turned[n + 2])
        total += jnp.where(column < NY - 1, pltpu.roll(tile, LANES - 1, 1), 0.0)
        total += jnp.where(column > 0, pltpu.roll(tile, 1, 1), 0.0)
        sums.append(total)
    return jnp.concatenate(sums, axis=1)


def smooth_kernel(place_ref, kappa_ref, own_ref, near_ref, far_ref, *refs):
    earlier, out_ref = refs[:-1], refs[-1]
    even = lax.rem(place_ref[3], 2) == 0
    own, near, far = [ref[...].astype(jnp.float32) for ref in (own_ref, near_ref, far_ref)]
    before, after = jnp.where(even, far, near), jnp.where(even, near, far)
    planes = [block[:, z] for block in (before, own, after) for z in range(own.shape[1])]
    for sweep in range(PASSES):
        scaled = [plane * kappa_ref[sweep + z, :][None] for z, plane in enumerate(planes)]
        planes = [
            planes[z] + (in_plane(scaled[z]) + scaled[z - 1] + scaled[z + 1] - 6.0 * scaled[z])
            for z in range(1, len(planes) - 1)
        ]
    for z in range(out_ref.shape[0]):
        rows = [ref[z] for ref in earlier] + [planes[z]]
        out_ref[z] = jnp.concatenate(rows).astype(out_ref.dtype)


def smooth(place, kappa_planes, group, earlier, kind):
    half, depth, plane = group[0].shape
    rows = half * (1 + len(earlier))
    operands = [keep(array) for array in group]
    return pl.pallas_call(
        smooth_kernel,
        out_shape=pltpu.VMEM((depth, rows, plane), kind),
        in_specs=[SMEM] + [VMEM] * (1 + len(operands) + len(earlier)),
        out_specs=VMEM,
        compiler_params=pltpu.CompilerParams(vmem_limit_bytes=16 << 20),
        cost_estimate=pl.CostEstimate(
            flops=100 * half * depth * plane, bytes_accessed=6 * half * depth * plane, transcendentals=0
        ),
        name="smooth",
    )(place, kappa_planes, *operands, *earlier)


def product_kernel(marks, norm_factor, last, place_ref, mine_ref, *refs):
    chips, chip, core, cell = place_ref[0], place_ref[1], place_ref[2], place_ref[3]
    depth = mine_ref.shape[0]
    sums, refs = refs[:last], refs[last:]
    sources = sum(len(slot) for slot in marks)
    inputs, outs = refs[:sources], refs[sources:]
    total = outs[0]
    if last:
        outs, total = outs[:-1], outs[-1]
        total[...] = sums[0][...]
    side = 2 * core - 1
    good = jnp.where(core == 0, chip > 0, chip < chips - 1)
    slots, targets, at = [], [], 0
    for slot in marks:
        refs, at = inputs[at : at + len(slot)], at + len(slot)
        indices = []
        for step, turned, other in slot:
            there = lax.rem(chip + (-side if turned else side) * step + chips, chips)
            indices.append(2 * there + (1 - core if other else core))
        if len(slot) == 1:
            slots.append([refs[0][z] for z in range(depth)])
            targets.append(indices[0])
        else:
            slots.append([jnp.where(good, refs[0][z], refs[1][z]) for z in range(depth)])
            targets.append(jnp.where(good, indices[0], indices[1]))
    value = sum(
        lax.dot_general(
            jnp.concatenate([slot[z] for slot in slots]), mine_ref[z], (((1,), (1,)), ((), ())),
            preferred_element_type=jnp.float32,
        )
        for z in range(depth)
    )
    rows = value.shape[0] // len(marks)
    for n, target in enumerate(targets):
        start = pl.multiple_of(target * rows, rows)
        total[pl.ds(start, rows), :] = value[n * rows : (n + 1) * rows] * norm_factor
    if last:
        part = outs[0].shape[0]
        for k, out in enumerate(outs):
            start = lax.rem(cell + k, len(outs)) * part
            out[...] = total[pl.ds(pl.multiple_of(start, part), part), :]


def product(place, mine, sums, slots, outs, norm_factor):
    depth, row_count, plane = mine.shape
    count = lax.axis_size("dp")
    rows = slots[0][0][0].shape[1]
    last = len(sums)
    out = pltpu.VMEM((count * rows // outs, row_count), jnp.float32)
    pairs = [pair for slot in slots for pair in slot]
    operands = [keep(array) for array, mark in pairs]
    marks = tuple(tuple(mark for _, mark in slot) for slot in slots)
    size = depth * plane
    need = 2 * size * (row_count + len(operands) * rows) + 4 * count * rows * row_count
    return pl.pallas_call(
        functools.partial(product_kernel, marks, norm_factor, last),
        out_shape=[out] * outs,
        in_specs=[SMEM] + [VMEM] * (1 + last + len(operands)),
        out_specs=[VMEM] * outs,
        scratch_shapes=[pltpu.VMEM((count * rows, row_count), jnp.float32)] * last,
        compiler_params=pltpu.CompilerParams(vmem_limit_bytes=need + (8 << 20)),
        cost_estimate=pl.CostEstimate(
            flops=2 * len(slots) * rows * row_count * size,
            bytes_accessed=2 * size * row_count,
            transcendentals=0,
        ),
        name="product",
    )(place, mine, *sums, *operands)


def swap_cores(block):
    return lax.ppermute(block, "dp", [(i, i ^ 1) for i in range(lax.axis_size("dp"))])


def first_rounds(block, mine):
    chips = lax.axis_size("dp") // 2
    ring = [(2 * i, 2 * ((i + 1) % chips)) for i in range(chips)]
    ring += [(2 * i + 1, 2 * ((i - 1) % chips) + 1) for i in range(chips)]
    both = [block, swap_cores(block)]
    slots = [[(both[0], (0, 0, 0))], [(both[1], (0, 0, 1))]]
    turned = []
    for step in range(1, chips // 2):
        both = [lax.ppermute(array, "dp", ring) for array in both]
        if step == 1:
            both[0], mine = lax.optimization_barrier((both[0], mine))
        slots += [[(both[0], (step, 0, 0))], [(both[1], (step, 0, 1))]]
        turned += [[(swap_cores(both[0]), (step, 1, 1))], [(swap_cores(both[1]), (step, 1, 0))]]
    if chips == 4:
        pairs = [(2, 4), (4, 6), (5, 3), (3, 1), (0, 2), (1, 0), (6, 7), (7, 5)]
    else:
        pairs = ring
    return slots, turned, [lax.ppermute(array, "dp", pairs) for array in both], mine


def last_round(both):
    chips = lax.axis_size("dp") // 2
    step = chips // 2
    if chips != 4:
        return [[(both[0], (step, 0, 0))], [(both[1], (step, 0, 1))]]
    turned = [swap_cores(array) for array in both]
    return [
        [(both[0], (step, 0, 0)), (turned[0], (step, 1, 1))],
        [(both[1], (step, 0, 1)), (turned[1], (step, 1, 0))],
    ]


def scatter_sum(parts):
    cells = len(parts)
    total = parts[0]
    for step in range(cells - 1, 0, -1):
        total += lax.ppermute(parts[step], "cell", [(i, (i + step) % cells) for i in range(cells)])
    return total


def on_device(sensitivity, kappa, pick_rows):
    row_count, slab_depth, plane_size = sensitivity.shape
    cells = lax.axis_size("cell")
    chips = lax.axis_size("dp") // 2
    slab_start = lax.axis_index("cell") * slab_depth
    norm_factor = 1.0 / math.sqrt(plane_size * slab_depth * cells)
    width = PASSES
    place = jnp.stack(
        [chips, lax.axis_index("dp") // 2, lax.axis_index("dp") % 2, lax.axis_index("cell")]
    ).astype(jnp.int32)
    kappa_planes = lax.dynamic_slice_in_dim(
        jnp.pad(kappa, ((width, width), (0, 0))), slab_start, slab_depth + 2 * width, 0
    )
    first, second = pick(sensitivity, pick_rows)
    second, kappa_planes = lax.optimization_barrier((second, kappa_planes))
    first, second = halo((first, second))
    half = smooth(place, kappa_planes, first, [], jnp.float32)
    smoothed = smooth(place, kappa_planes, second, [half], sensitivity.dtype)
    smoothed, sensitivity = lax.optimization_barrier((smoothed, sensitivity))
    early, turned, both, mine = first_rounds(smoothed, sensitivity.transpose(1, 0, 2))
    sums = product(place, mine, [], early, 1, norm_factor)
    both[1], sums = lax.optimization_barrier((both[1], sums))
    parts = product(place, mine, sums, turned + last_round(both), cells, norm_factor)
    return scatter_sum(parts).T


def solution(mesh):
    placed = (P("dp", "cell"), P(), P("dp"))
    return jax.shard_map(
        on_device, mesh=mesh, in_specs=placed, out_specs=P("dp", "cell"), check_vma=False
    )
```
